512 devices in a mesh: chan: 16 (over y, core), space: 8 (over z), sample: 4 (over x).
Axes of the slice: x: 4, y: 8, z: 8, core: 2. Of those that a mesh axis runs over, the one named last changes fastest.
Arguments:
- inputs: bfloat16 [4, 128, 16, 4096], P('sample', 'chan', 'space'), may hold values from -6 to 6
- weights: bfloat16 [27, 128, 128], P(None, 'chan'), may hold values from -0.125 to 0.125
- grad_out: bfloat16 [4, 128, 16, 4096], P('sample', 'chan', 'space'), may hold values from -6 to 6
Outputs:
- output: bfloat16 [4, 128, 16, 4096], P('sample', 'chan', 'space')
- grad_in: bfloat16 [4, 128, 16, 4096], P('sample', 'chan', 'space')
- grad_weights: float32 [27, 128, 128], P(None, 'chan')
The draws below stay inside these ranges and needn't reach their ends.
All inputs are finite; a program needn't handle non-finite values.
Results may differ from the reference program's by a relative error of at most 0.001.
Values may be sent and summed in bfloat16 or wider, within the bound.
No kernel may reach another device: no remote copies, remote signals or barrier semaphores. Data moves between devices by JAX's collectives and lax.ppermute only.
A program may use at most 64 MiB of HBM per device.

```python
import math
import jax
import jax.numpy as jnp
from jax import lax

C = 128
O = 128
TAPS = 27
SIDE = 64
HW = 4096
DEPTH = 16
BATCH = 4
VOXELS = 262144


def spiked(entries, own_key, source, target, parts, factor):
    owner, partner = [(jnp.arange(entries.shape[axis_at]) // (entries.shape[axis_at] // parts)).reshape([-1 if axis == axis_at else 1 for axis in range(entries.ndim)]) for axis_at in (source, target)]
    chosen = jax.random.permutation(own_key, parts)[partner]
    strong = (owner == chosen) | (owner == (partner + parts // 2) % parts)
    return jnp.where(strong, factor * entries, entries)


def block_scale(own_key, extent, pieces, low, top_value):
    def one(dim, shards_of):
        draws = jax.random.uniform(jax.random.fold_in(jax.random.fold_in(own_key, 6), dim), (shards_of,), jnp.float32, low / len(pieces), top_value / len(pieces))
        return jnp.repeat(jnp.exp(draws), extent[dim] // shards_of).reshape((-1,) + (1,) * (len(extent) - dim - 1))

    loudness = one(*pieces[0])
    for cut in pieces[1:]:
        loudness = loudness * one(*cut)
    return loudness


def scatter_about(stream_key, extent, spread, reach, pieces=(), kind=jnp.bfloat16):
    loudness = block_scale(stream_key, extent, pieces, -0.22, 0.18) if pieces else 1.0
    array = jax.random.normal(stream_key, extent, jnp.float32) * spread * loudness
    return jnp.minimum(jnp.maximum(array, -reach), reach).astype(kind)


def heavy_noise(rng, shape, spread, most, cuts, heavy, kind=jnp.bfloat16):
    drawn = spread * jax.random.normal(rng, shape, jnp.float32)
    if cuts:
        drawn = drawn * block_scale(rng, shape, cuts, -0.22, 0.18)
    return jnp.clip(spiked(drawn, jax.random.fold_in(rng, 3), *heavy), -most, most).astype(kind)


def setup_inputs(seed: int = 0) -> dict:
    splits = jax.random.split(jax.random.key(seed), 4)
    return {
        "inputs": scatter_about(splits[0], (BATCH, C, DEPTH, HW), 1.0, 6.0, ((0, 4), (1, 16), (2, 8))),
        "weights": heavy_noise(splits[1], (TAPS, C, O), (TAPS * C) ** -0.5, 0.125, ((1, 16),), (1, 2, 16, 2.0)),
        "grad_out": scatter_about(splits[2], (BATCH, O, DEPTH, HW), 1.0, 6.0, ((0, 4), (1, 16), (2, 8))),
    }


def convolve(volume, kernel):
    return lax.conv_general_dilated(volume, kernel, (1, 1, 1), [(1, 1), (1, 1), (1, 1)], dimension_numbers=('NCDHW', 'DHWIO', 'NCDHW'), precision=lax.Precision.HIGHEST)

def reference(inputs, weights, grad_out):
    volume = inputs.astype(jnp.float32).reshape(BATCH, C, DEPTH, SIDE, SIDE)
    kernel = weights.astype(jnp.float32).reshape(3, 3, 3, C, O)
    gradient = grad_out.astype(jnp.float32).reshape(BATCH, O, DEPTH, SIDE, SIDE)
    summed, pullback = jax.vjp(convolve, volume, kernel)
    output = summed.astype(jnp.bfloat16).reshape(BATCH, O, DEPTH, HW)
    grad_volume, grad_kernel = pullback(gradient)
    grad_in = grad_volume.astype(jnp.bfloat16).reshape(BATCH, C, DEPTH, HW)
    grad_weights = (grad_kernel * (1.0 / math.sqrt(VOXELS))).reshape(TAPS, C, O).astype(jnp.float32)
    return (output, grad_in, grad_weights)
```

```python
import math

import jax
import jax.numpy as jnp
from jax import lax
from jax.experimental import pallas as pl
from jax.experimental.pallas import tpu as pltpu
from jax.sharding import PartitionSpec as P

SIDE = 64
BF16 = jnp.bfloat16
F32 = jnp.float32
VMEM = pltpu.CompilerParams(vmem_limit_bytes=48 * 1024 * 1024)


def rolled(block, amount):
    return pltpu.roll(block, amount % block.shape[-1], axis=block.ndim - 1)


def lane_index(shape):
    return lax.broadcasted_iota(jnp.int32, shape, len(shape) - 1)


def shift_rows(block, rows):
    cells = block.shape[-1]
    lane = lane_index(block.shape) + rows * SIDE
    moved = rolled(block, -rows * SIDE)
    return jnp.where((lane >= 0) & (lane < cells), moved, 0.0)


def shift_cols(block, cols):
    col = lane_index(block.shape) % SIDE + cols
    moved = rolled(block, -cols)
    return jnp.where((col >= 0) & (col < SIDE), moved, 0.0)


def strips_kernel(x_ref, g_ref, out_ref):
    strips = out_ref.shape[0] // 2
    cells = x_ref.shape[1] // 2
    inner = cells // strips
    width = inner + 2 * SIDE
    for which, ref in enumerate((x_ref, g_ref)):
        for plane in range(2):
            block = ref[:, plane * cells : (plane + 1) * cells].astype(F32)
            zeros = jnp.zeros((block.shape[0], 2 * SIDE), F32)
            wide = rolled(jnp.concatenate([block, zeros], axis=1), SIDE).astype(BF16)
            for strip in range(strips):
                out_ref[2 * strip + which, :, plane * width : (plane + 1) * width] = wide[
                    :, strip * inner : strip * inner + width
                ]


def kernel_grad_kernel(x_ref, low_ref, high_ref, g_ref, out_ref, xs, gs):
    cells = low_ref.shape[1]
    c_rows, o_rows = x_ref.shape[0], g_ref.shape[0]
    for plane in range(4):
        if plane == 0:
            block = low_ref[...]
        elif plane == 3:
            block = high_ref[...]
        else:
            block = x_ref[:, (plane - 1) * cells : plane * cells]
        wide = block.astype(F32)
        first = 3 * plane * c_rows
        xs[first : first + c_rows] = shift_rows(wide, -1).astype(BF16)
        xs[first + c_rows : first + 2 * c_rows] = block
        xs[first + 2 * c_rows : first + 3 * c_rows] = shift_rows(wide, 1).astype(BF16)
    total = jnp.zeros((9 * c_rows, 3 * o_rows), F32)
    for plane in range(2):
        block = g_ref[:, plane * cells : (plane + 1) * cells]
        wide = block.astype(F32)
        gs[0:o_rows] = shift_cols(wide, 1).astype(BF16)
        gs[o_rows : 2 * o_rows] = block
        gs[2 * o_rows : 3 * o_rows] = shift_cols(wide, -1).astype(BF16)
        first = 3 * plane * c_rows
        total = total + lax.dot_general(
            xs[first : first + 9 * c_rows],
            gs[...],
            (((1,), (1,)), ((), ())),
            preferred_element_type=F32,
        )
    parts = out_ref.shape[0]
    rows = c_rows // parts
    for part in range(parts):
        for tap in range(9):
            start = tap * c_rows + part * rows
            out_ref[part, tap * rows : (tap + 1) * rows, :] = total[start : start + rows]


def filter_order_kernel(parts_ref, out_ref):
    parts, rows, _ = parts_ref.shape
    o_rows = parts_ref.shape[2] // 3
    c_rows = out_ref.shape[1]
    out_all = out_ref.shape[2]
    chunk = o_rows // parts
    source = lax.broadcasted_iota(jnp.int32, (3 * o_rows, out_all), 0)
    target = lax.broadcasted_iota(jnp.int32, (3 * o_rows, out_all), 1)
    for col_k in range(3):
        placed = jnp.zeros((rows, out_all), F32)
        for part in range(parts):
            local_o = source - col_k * o_rows
            home = (lax.div(local_o, chunk) * parts + part) * chunk + lax.rem(local_o, chunk)
            chosen = (local_o >= 0) & (local_o < o_rows) & (home == target)
            placed = placed + lax.dot_general(
                parts_ref[part],
                jnp.where(chosen, 1.0, 0.0).astype(F32),
                (((1,), (0,)), ((), ())),
                precision=lax.Precision.HIGHEST,
                preferred_element_type=F32,
            )
        for tap in range(9):
            out_ref[3 * tap + col_k] = placed[tap * c_rows : (tap + 1) * c_rows]
    for spare in range(27, out_ref.shape[0]):
        out_ref[spare] = jnp.zeros(out_ref.shape[1:], F32)


def convolve_kernel(which_ref, d_ref, low_ref, high_ref, w_ref, out_ref, cols):
    channels, width = low_ref.shape
    inner = width - 2 * SIDE
    for plane in range(4):
        if plane == 0:
            block = low_ref[...]
        elif plane == 3:
            block = high_ref[...]
        else:
            block = d_ref[:, (plane - 1) * width : plane * width]
        wide = block.astype(F32)
        for col_k in range(3):
            moved = wide if col_k == 1 else shift_cols(wide, col_k - 1)
            middle = rolled(moved, -SIDE).astype(BF16)[:, :inner]
            ends = moved.astype(BF16)
            pieces = (ends[:, :inner], middle, ends[:, 2 * SIDE :])
            for row_k in range(3):
                first = (3 * row_k + col_k) * channels
                cols[first : first + channels, plane * inner : (plane + 1) * inner] = pieces[row_k]

    @pl.when(which_ref[0] == 0)
    def _():
        total = jnp.zeros(out_ref.shape, F32)
        for plane_k in range(3):
            total = total + lax.dot_general(
                w_ref[9 * plane_k * channels : 9 * (plane_k + 1) * channels],
                cols[:, plane_k * inner : (plane_k + 2) * inner],
                (((0,), (0,)), ((), ())),
                preferred_element_type=F32,
            )
        out_ref[...] = total.astype(BF16)

    @pl.when(which_ref[0] == 1)
    def _():
        total = jnp.zeros(out_ref.shape, F32)
        for plane_k in range(3):
            taps = [26 - 9 * plane_k - tap for tap in range(9)]
            mirrored = jnp.concatenate(
                [w_ref[tap * channels : (tap + 1) * channels] for tap in taps], axis=1
            )
            total = total + jnp.dot(
                mirrored,
                cols[:, plane_k * inner : (plane_k + 2) * inner],
                preferred_element_type=F32,
            )
        out_ref[...] = total.astype(BF16)


def local(inputs, weights, grad_out):
    _, c_dev, planes, cells = inputs.shape
    out_all = weights.shape[2]
    n_chan = lax.axis_size("chan")
    n_space = lax.axis_size("space")
    n_batch = lax.axis_size("sample")
    group = 4
    strips = n_chan // 2
    inner = cells // strips
    width = inner + 2 * SIDE
    side_by_side = [[group * i + j for j in range(group)] for i in range(n_chan // group)]
    strided = [[group * i + j for i in range(n_chan // group)] for j in range(group)]
    forward = [(i, i + 1) for i in range(n_space - 1)]
    backward = [(target, source) for source, target in forward]
    which = lax.rem(lax.axis_index("chan"), 2)
    whole = pl.BlockSpec(memory_space=pltpu.VMEM)

    x = inputs.reshape(c_dev, planes * cells)
    g = grad_out.reshape(c_dev, planes * cells)

    x_block = lax.all_to_all(
        jnp.broadcast_to(x, (group, *x.shape)), "chan", 0, 0, axis_index_groups=side_by_side
    ).reshape(group * c_dev, planes * cells)
    g_block = lax.all_to_all(
        jnp.broadcast_to(g, (group, *g.shape)), "chan", 0, 0, axis_index_groups=strided
    ).reshape(group * c_dev, planes * cells)

    strip_parts = pl.pallas_call(
        strips_kernel,
        out_shape=jax.ShapeDtypeStruct((n_chan, c_dev, planes * width), BF16),
        in_specs=[whole, whole],
        out_specs=whole,
        compiler_params=VMEM,
    )(x, g)
    strip = lax.all_to_all(strip_parts, "chan", 0, 0).reshape(n_chan * c_dev, planes * width)
    all_weights = lax.all_gather(weights, "chan", axis=1, tiled=True)

    low = lax.ppermute(x_block[:, cells:], "space", forward)
    high = lax.ppermute(x_block[:, :cells], "space", backward)
    block = group * c_dev
    terms = pl.pallas_call(
        kernel_grad_kernel,
        out_shape=jax.ShapeDtypeStruct((group, 9 * c_dev, 3 * block), F32),
        in_specs=[whole] * 4,
        out_specs=whole,
        scratch_shapes=[
            pltpu.VMEM((12 * block, cells), BF16),
            pltpu.VMEM((3 * block, cells), BF16),
        ],
        compiler_params=VMEM,
    )(x_block, low, high, g_block)
    terms = lax.all_to_all(terms, "chan", 0, 0, axis_index_groups=side_by_side)
    shares = n_space * n_batch
    terms = pl.pallas_call(
        filter_order_kernel,
        out_shape=jax.ShapeDtypeStruct((shares, c_dev, out_all), F32),
        in_specs=[whole],
        out_specs=whole,
        compiler_params=VMEM,
    )(terms)
    scale = 1.0 / math.sqrt(shares * planes * cells)
    terms = lax.all_to_all(terms, ("space", "sample"), 0, 0)
    share = jnp.sum(terms, axis=0, keepdims=True) * scale
    shared = lax.all_to_all(jnp.broadcast_to(share, terms.shape), ("space", "sample"), 0, 0)
    grad_weights = shared[: weights.shape[0]]

    strip_low = lax.ppermute(strip[:, width:], "space", forward)
    strip_high = lax.ppermute(strip[:, :width], "space", backward)
    result = pl.pallas_call(
        convolve_kernel,
        out_shape=jax.ShapeDtypeStruct((n_chan * c_dev, planes * inner), BF16),
        in_specs=[pl.BlockSpec(memory_space=pltpu.SMEM)] + [whole] * 4,
        out_specs=whole,
        scratch_shapes=[pltpu.VMEM((9 * n_chan * c_dev, 4 * inner), BF16)],
        compiler_params=VMEM,
    )(
        which.reshape(1),
        strip,
        strip_low,
        strip_high,
        all_weights.reshape(27 * n_chan * c_dev, out_all),
    )
    back = lax.all_to_all(result.reshape(n_chan, c_dev, planes * inner), "chan", 0, 0)
    back = back.reshape(strips, 2, c_dev, planes, inner).transpose(1, 2, 3, 0, 4)
    back = back.reshape(2, 1, c_dev, planes, cells)
    return back[0], back[1], grad_weights


def solution(mesh):
    in_specs = (
        P("sample", "chan", "space", None),
        P(None, "chan", None),
        P("sample", "chan", "space", None),
    )
    out_specs = (
        P("sample", "chan", "space", None),
        P("sample", "chan", "space", None),
        P(None, "chan", None),
    )
    return jax.shard_map(local, mesh=mesh, in_specs=in_specs, out_specs=out_specs, check_vma=False)
```

```python
import math

import jax
import jax.numpy as jnp
from jax import lax
from jax.experimental import pallas as pl
from jax.experimental.pallas import tpu as pltpu
from jax.sharding import PartitionSpec as P

SIDE = 64
BF16 = jnp.bfloat16
F32 = jnp.float32
VMEM = pltpu.CompilerParams(vmem_limit_bytes=48 * 1024 * 1024)


def rolled(block, amount):
    return pltpu.roll(block, amount % block.shape[-1], axis=block.ndim - 1)


def lane_index(shape):
    return lax.broadcasted_iota(jnp.int32, shape, len(shape) - 1)


def shift_rows(block, rows):
    cells = block.shape[-1]
    lane = lane_index(block.shape) + rows * SIDE
    moved = rolled(block, -rows * SIDE)
    return jnp.where((lane >= 0) & (lane < cells), moved, 0.0)


def shift_cols(block, cols):
    col = lane_index(block.shape) % SIDE + cols
    moved = rolled(block, -cols)
    return jnp.where((col >= 0) & (col < SIDE), moved, 0.0)


def chip_block(which_ref, own_ref, other_ref, chip, start, stop):
    own = own_ref[chip, :, start:stop].astype(F32)
    other = other_ref[chip, :, start:stop].astype(F32)
    even = which_ref[0] == 0
    return jnp.concatenate(
        [jnp.where(even, own, other), jnp.where(even, other, own)], axis=0
    )


def send_kernel(x_ref, g_ref, w_ref, row_ref, gs_ref):
    cells = x_ref.shape[1]
    row_ref[:, :cells] = x_ref[...]
    taps, _, out_all = w_ref.shape
    for tap in range(taps):
        start = cells + tap * out_all
        row_ref[:, start : start + out_all] = w_ref[tap]
    for chip in range(gs_ref.shape[0]):
        gs_ref[chip] = g_ref[...]


def kernel_grad_kernel(which_ref, x_ref, low_ref, high_ref, own_ref, other_ref, out_ref, gs):
    cells = low_ref.shape[1]
    chips, c_rows, _ = own_ref.shape
    out_all = 2 * chips * c_rows
    planes = [low_ref[...], x_ref[:, :cells], x_ref[:, cells : 2 * cells], high_ref[...]]
    moved = []
    for block in planes:
        wide = block.astype(F32)
        moved.append([shift_rows(wide, -1), wide, shift_rows(wide, 1)])
    total = jnp.zeros((9 * c_rows, 3 * out_all), F32)
    for plane in range(2):
        rows = [moved[plane + plane_k][row_k] for plane_k in range(3) for row_k in range(3)]
        for chip in range(chips):
            block = chip_block(
                which_ref, own_ref, other_ref, chip, plane * cells, (plane + 1) * cells
            )
            for col_k in range(3):
                first = col_k * out_all + 2 * c_rows * chip
                turned = block if col_k == 1 else shift_cols(block, 1 - col_k)
                gs[first : first + 2 * c_rows] = turned.astype(BF16)
        total = total + lax.dot_general(
            jnp.concatenate(rows, axis=0).astype(BF16),
            gs[...],
            (((1,), (1,)), ((), ())),
            preferred_element_type=F32,
        )
    for tap in range(9):
        for col_k in range(3):
            out_ref[3 * tap + col_k] = total[
                tap * c_rows : (tap + 1) * c_rows, col_k * out_all : (col_k + 1) * out_all
            ]
    for spare in range(27, out_ref.shape[0]):
        out_ref[spare] = jnp.zeros(out_ref.shape[1:], F32)


def convolve_kernel(
    me_ref, which_ref, all_ref, own_ref, other_ref, w_ref, after_ref,
    middle_ref, low_ref, high_ref, g_all, terms,
):
    del after_ref
    rows, out_all = w_ref.shape
    taps = 27
    c_rows = rows // taps
    cells = low_ref.shape[1]
    wide = 2 * cells
    channel = lax.broadcasted_iota(jnp.int32, (c_rows, out_all), 0) + c_rows * me_ref[0]
    mine = jnp.where(channel == lax.broadcasted_iota(jnp.int32, (c_rows, out_all), 1), 1.0, 0.0)
    picked = []
    for tap in reversed(range(taps)):
        start = wide + tap * out_all
        picked.append(
            lax.dot_general(
                mine.astype(BF16),
                all_ref[:, start : start + out_all],
                (((1,), (1,)), ((), ())),
                preferred_element_type=F32,
            )
        )
    kernels = (jnp.concatenate(picked, axis=0).astype(BF16), w_ref[...])
    for which in range(2):
        home = slice(which * c_rows, (which + 1) * c_rows)
        for plane in range(2):
            span = slice(plane * cells, (plane + 1) * cells)
            if which == 0:
                block = all_ref[:, span]
            else:
                for chip in range(own_ref.shape[0]):
                    g_all[2 * c_rows * chip : 2 * c_rows * (chip + 1)] = chip_block(
                        which_ref, own_ref, other_ref, chip, span.start, span.stop
                    ).astype(BF16)
                block = g_all[...]
            terms[plane] = jnp.dot(kernels[which], block, preferred_element_type=F32)
        for target in range(4):
            result = jnp.zeros((c_rows, cells), F32)
            for col_k in range(3):
                column = jnp.zeros((c_rows, cells), F32)
                for row_k in range(3):
                    sums = jnp.zeros((c_rows, cells), F32)
                    for plane in range(2):
                        plane_k = target - plane
                        if 0 <= plane_k < 3:
                            first = c_rows * (9 * plane_k + 3 * row_k + col_k)
                            sums = sums + terms[plane, first : first + c_rows]
                    column = column + (sums if row_k == 1 else shift_rows(sums, 1 - row_k))
                result = result + (column if col_k == 1 else shift_cols(column, 1 - col_k))
            if target == 0:
                low_ref[home] = result
            elif target == 3:
                high_ref[home] = result
            else:
                middle_ref[target - 1, home] = result


def call(kernel, out_shape, scratch_shapes, *args, after=None):
    whole = pl.BlockSpec(memory_space=pltpu.VMEM)
    scalars = pl.BlockSpec(memory_space=pltpu.SMEM)
    in_specs = [scalars if arg.dtype == jnp.int32 else whole for arg in args]
    if after is not None:
        in_specs.append(pl.BlockSpec(memory_space=pl.ANY))
        args = (*args, after)
    return pl.pallas_call(
        kernel,
        out_shape=out_shape,
        in_specs=in_specs,
        out_specs=jax.tree.map(lambda _: whole, out_shape),
        scratch_shapes=scratch_shapes,
        compiler_params=VMEM,
    )(*args)


def local(inputs, weights, grad_out):
    _, c_dev, planes, cells = inputs.shape
    taps, _, out_all = weights.shape
    n_chan = lax.axis_size("chan")
    n_space = lax.axis_size("space")
    n_batch = lax.axis_size("sample")
    chips = n_chan // 2
    along_y = [[core + 2 * chip for chip in range(chips)] for core in range(2)]
    cores = [(i, i ^ 1) for i in range(n_chan)]
    forward = [(i, i + 1) for i in range(n_space - 1)]
    backward = [(target, source) for source, target in forward]
    me = lax.axis_index("chan").reshape(1)
    which = lax.rem(me, 2)
    shape = jax.ShapeDtypeStruct

    x = inputs.reshape(c_dev, planes * cells)
    g = grad_out.reshape(c_dev, planes * cells)
    row, g_copies = call(
        send_kernel,
        (
            shape((c_dev, planes * cells + taps * out_all), BF16),
            shape((chips, c_dev, planes * cells), BF16),
        ),
        [],
        x, g, weights,
    )
    gathered = lax.all_gather(row, "chan", axis=0, tiled=True)
    own = lax.all_to_all(g_copies, "chan", 0, 0, axis_index_groups=along_y)
    x_low = lax.ppermute(x[:, cells:], "space", forward)
    x_high = lax.ppermute(x[:, :cells], "space", backward)
    own, x_low, x_high = lax.optimization_barrier((own, x_low, x_high))
    other = lax.ppermute(own, "chan", cores)

    shares = n_space * n_batch
    terms = call(
        kernel_grad_kernel,
        shape((shares, c_dev, out_all), F32),
        [pltpu.VMEM((3 * out_all, cells), BF16)],
        which, x, x_low, x_high, own, other,
    )
    partial = terms
    terms = lax.all_to_all(terms, ("space", "sample"), 0, 0)

    middle, to_below, to_above = call(
        convolve_kernel,
        (
            shape((planes, 2 * c_dev, cells), F32),
            shape((2 * c_dev, cells), F32),
            shape((2 * c_dev, cells), F32),
        ),
        [pltpu.VMEM((out_all, cells), BF16), pltpu.VMEM((planes, taps * c_dev, cells), F32)],
        me, which, gathered, own, other, weights.reshape(taps * c_dev, out_all),
        after=partial,
    )
    scale = 1.0 / math.sqrt(shares * planes * cells)
    terms, middle = lax.optimization_barrier((terms, middle))
    share = jnp.sum(terms, axis=0, keepdims=True) * scale
    shared = lax.all_to_all(jnp.broadcast_to(share, terms.shape), ("space", "sample"), 0, 0)
    grad_weights = shared[:taps]

    from_below = lax.ppermute(to_above, "space", forward)
    from_above = lax.ppermute(to_below, "space", backward)
    both = jnp.stack([middle[0] + from_below, middle[1] + from_above], 1).astype(BF16)
    return both[None, :c_dev], both[None, c_dev:], grad_weights


def solution(mesh):
    in_specs = (
        P("sample", "chan", "space", None),
        P(None, "chan", None),
        P("sample", "chan", "space", None),
    )
    out_specs = (
        P("sample", "chan", "space", None),
        P("sample", "chan", "space", None),
        P(None, "chan", None),
    )
    return jax.shard_map(local, mesh=mesh, in_specs=in_specs, out_specs=out_specs, check_vma=False)
```

```python
import math

import jax
import jax.numpy as jnp
from jax import lax
from jax.experimental import pallas as pl
from jax.experimental.pallas import tpu as pltpu
from jax.sharding import PartitionSpec as P

SIDE = 64
BF16 = jnp.bfloat16
F32 = jnp.float32
VMEM = pltpu.CompilerParams(vmem_limit_bytes=48 * 1024 * 1024)


def rolled(block, amount):
    return pltpu.roll(block, amount % block.shape[-1], axis=block.ndim - 1)


def lane_index(shape):
    return lax.broadcasted_iota(jnp.int32, shape, len(shape) - 1)


def shift_rows(block, rows):
    cells = block.shape[-1]
    lane = lane_index(block.shape) + rows * SIDE
    moved = rolled(block, -rows * SIDE)
    return jnp.where((lane >= 0) & (lane < cells), moved, 0.0)


def shift_cols(block, cols):
    col = lane_index(block.shape) % SIDE + cols
    moved = rolled(block, -cols)
    return jnp.where((col >= 0) & (col < SIDE), moved, 0.0)


def chip_block(which_ref, own_ref, other_ref, chip, start, stop):
    own = own_ref[chip, :, start:stop].astype(F32)
    other = other_ref[chip, :, start:stop].astype(F32)
    even = which_ref[0] == 0
    return jnp.concatenate(
        [jnp.where(even, own, other), jnp.where(even, other, own)], axis=0
    )


def send_kernel(x_ref, g_ref, w_ref, row_ref, gs_ref):
    cells = x_ref.shape[1]
    row_ref[:, :cells] = x_ref[...]
    taps, _, out_all = w_ref.shape
    for tap in range(taps):
        start = cells + tap * out_all
        row_ref[:, start : start + out_all] = w_ref[tap]
    for chip in range(gs_ref.shape[0]):
        gs_ref[chip] = g_ref[...]


def kernel_grad_kernel(which_ref, x_ref, low_ref, high_ref, own_ref, other_ref, out_ref, gs):
    cells = low_ref.shape[1]
    chips, c_rows, _ = own_ref.shape
    out_all = 2 * chips * c_rows
    planes = [low_ref[...], x_ref[:, :cells], x_ref[:, cells : 2 * cells], high_ref[...]]
    moved = []
    for block in planes:
        wide = block.astype(F32)
        moved.append([shift_rows(wide, -1), wide, shift_rows(wide, 1)])
    total = jnp.zeros((9 * c_rows, 3 * out_all), F32)
    for plane in range(2):
        rows = [moved[plane + plane_k][row_k] for plane_k in range(3) for row_k in range(3)]
        for chip in range(chips):
            block = chip_block(
                which_ref, own_ref, other_ref, chip, plane * cells, (plane + 1) * cells
            )
            for col_k in range(3):
                first = col_k * out_all + 2 * c_rows * chip
                turned = block if col_k == 1 else shift_cols(block, 1 - col_k)
                gs[first : first + 2 * c_rows] = turned.astype(BF16)
        total = total + lax.dot_general(
            jnp.concatenate(rows, axis=0).astype(BF16),
            gs[...],
            (((1,), (1,)), ((), ())),
            preferred_element_type=F32,
        )
    for tap in range(9):
        for col_k in range(3):
            out_ref[3 * tap + col_k] = total[
                tap * c_rows : (tap + 1) * c_rows, col_k * out_all : (col_k + 1) * out_all
            ]
    for spare in range(27, out_ref.shape[0]):
        out_ref[spare] = jnp.zeros(out_ref.shape[1:], F32)


def convolve_kernel(
    me_ref, which_ref, all_ref, own_ref, other_ref, w_ref, after_ref,
    middle_ref, low_ref, high_ref, g_all, terms,
):
    del after_ref
    rows, out_all = w_ref.shape
    taps = 27
    c_rows = rows // taps
    cells = low_ref.shape[1]
    wide = 2 * cells
    channel = lax.broadcasted_iota(jnp.int32, (c_rows, out_all), 0) + c_rows * me_ref[0]
    mine = jnp.where(channel == lax.broadcasted_iota(jnp.int32, (c_rows, out_all), 1), 1.0, 0.0)
    picked = []
    for tap in reversed(range(taps)):
        start = wide + tap * out_all
        picked.append(
            lax.dot_general(
                mine.astype(BF16),
                all_ref[:, start : start + out_all],
                (((1,), (1,)), ((), ())),
                preferred_element_type=F32,
            )
        )
    kernels = (jnp.concatenate(picked, axis=0).astype(BF16), w_ref[...])
    for which in range(2):
        home = slice(which * c_rows, (which + 1) * c_rows)
        for plane in range(2):
            span = slice(plane * cells, (plane + 1) * cells)
            if which == 0:
                block = all_ref[:, span]
            else:
                for chip in range(own_ref.shape[0]):
                    g_all[2 * c_rows * chip : 2 * c_rows * (chip + 1)] = chip_block(
                        which_ref, own_ref, other_ref, chip, span.start, span.stop
                    ).astype(BF16)
                block = g_all[...]
            terms[plane] = jnp.dot(kernels[which], block, preferred_element_type=F32)
        for target in range(4):
            result = jnp.zeros((c_rows, cells), F32)
            for col_k in range(3):
                column = jnp.zeros((c_rows, cells), F32)
                for row_k in range(3):
                    sums = jnp.zeros((c_rows, cells), F32)
                    for plane in range(2):
                        plane_k = target - plane
                        if 0 <= plane_k < 3:
                            first = c_rows * (9 * plane_k + 3 * row_k + col_k)
                            sums = sums + terms[plane, first : first + c_rows]
                    column = column + (sums if row_k == 1 else shift_rows(sums, 1 - row_k))
                result = result + (column if col_k == 1 else shift_cols(column, 1 - col_k))
            if target == 0:
                low_ref[home] = result
            elif target == 3:
                high_ref[home] = result
            else:
                middle_ref[target - 1, home] = result


def call(kernel, out_shape, scratch_shapes, *args, after=None, flops=None):
    whole = pl.BlockSpec(memory_space=pltpu.VMEM)
    scalars = pl.BlockSpec(memory_space=pltpu.SMEM)
    in_specs = [scalars if arg.dtype == jnp.int32 else whole for arg in args]
    if after is not None:
        in_specs.append(pl.BlockSpec(memory_space=pl.ANY))
        args = (*args, after)
    return pl.pallas_call(
        kernel,
        out_shape=out_shape,
        in_specs=in_specs,
        out_specs=jax.tree.map(lambda _: whole, out_shape),
        scratch_shapes=scratch_shapes,
        compiler_params=VMEM,
        cost_estimate=flops and pl.CostEstimate(flops=flops, bytes_accessed=0, transcendentals=0),
    )(*args)


def finish_kernel(middle_ref, below_ref, above_ref, out_ref, grad_ref):
    rows = out_ref.shape[0]
    for home, ref in ((slice(0, rows), out_ref), (slice(rows, 2 * rows), grad_ref)):
        first = middle_ref[0, home] + below_ref[home]
        second = middle_ref[1, home] + above_ref[home]
        ref[...] = jnp.stack([first, second], axis=1).astype(BF16)


def take_kernel(shares_ref, out_ref):
    out_ref[...] = shares_ref[: out_ref.shape[0]]


def local(inputs, weights, grad_out):
    _, c_dev, planes, cells = inputs.shape
    taps, _, out_all = weights.shape
    n_chan = lax.axis_size("chan")
    n_space = lax.axis_size("space")
    n_batch = lax.axis_size("sample")
    chips = n_chan // 2
    along_y = [[core + 2 * chip for chip in range(chips)] for core in range(2)]
    cores = [(i, i ^ 1) for i in range(n_chan)]
    forward = [(i, i + 1) for i in range(n_space - 1)]
    backward = [(target, source) for source, target in forward]
    me = lax.axis_index("chan").reshape(1)
    which = lax.rem(me, 2)
    shape = jax.ShapeDtypeStruct

    x = inputs.reshape(c_dev, planes * cells)
    g = grad_out.reshape(c_dev, planes * cells)
    row, g_copies = call(
        send_kernel,
        (
            shape((c_dev, planes * cells + taps * out_all), BF16),
            shape((chips, c_dev, planes * cells), BF16),
        ),
        [],
        x, g, weights,
    )
    gathered = lax.all_gather(row, "chan", axis=0, tiled=True)
    own = lax.all_to_all(g_copies, "chan", 0, 0, axis_index_groups=along_y)
    x_low = lax.ppermute(x[:, cells:], "space", forward)
    x_high = lax.ppermute(x[:, :cells], "space", backward)
    own, x_low, x_high = lax.optimization_barrier((own, x_low, x_high))
    other = lax.ppermute(own, "chan", cores)

    shares = n_space * n_batch
    terms = call(
        kernel_grad_kernel,
        shape((shares, c_dev, out_all), F32),
        [pltpu.VMEM((3 * out_all, cells), BF16)],
        which, x, x_low, x_high, own, other,
    )
    partial = terms
    terms = lax.all_to_all(terms, ("space", "sample"), 0, 0)

    middle, to_below, to_above = call(
        convolve_kernel,
        (
            shape((planes, 2 * c_dev, cells), F32),
            shape((2 * c_dev, cells), F32),
            shape((2 * c_dev, cells), F32),
        ),
        [pltpu.VMEM((out_all, cells), BF16), pltpu.VMEM((planes, taps * c_dev, cells), F32)],
        me, which, gathered, own, other, weights.reshape(taps * c_dev, out_all),
        after=partial,
    )
    scale = 1.0 / math.sqrt(shares * planes * cells)
    terms, middle = lax.optimization_barrier((terms, middle))
    share = jnp.sum(terms, axis=0, keepdims=True) * scale
    spread = jnp.broadcast_to(share, terms.shape)
    spread, to_above, to_below = lax.optimization_barrier((spread, to_above, to_below))
    shared = lax.all_to_all(spread, ("space", "sample"), 0, 0)
    grad_weights = call(
        take_kernel, shape(weights.shape, F32), [], shared, flops=30_000_000_000
    )

    from_below = lax.ppermute(to_above, "space", forward)
    from_above = lax.ppermute(to_below, "space", backward)
    output, grad_in = call(
        finish_kernel, (shape(inputs.shape[1:], BF16),) * 2, [], middle, from_below, from_above
    )
    return output[None], grad_in[None], grad_weights


def solution(mesh):
    in_specs = (
        P("sample", "chan", "space", None),
        P(None, "chan", None),
        P("sample", "chan", "space", None),
    )
    out_specs = (
        P("sample", "chan", "space", None),
        P("sample", "chan", "space", None),
        P(None, "chan", None),
    )
    return jax.shard_map(local, mesh=mesh, in_specs=in_specs, out_specs=out_specs, check_vma=False)
```

```python
import functools
import math

import jax
import jax.numpy as jnp
from jax import lax
from jax.experimental import pallas as pl
from jax.experimental.pallas import tpu as pltpu
from jax.sharding import PartitionSpec as P

SIDE = 64
BF16 = jnp.bfloat16
F32 = jnp.float32
MIB = 1024 * 1024


def rolled(block, amount):
    return pltpu.roll(block, amount % block.shape[-1], axis=block.ndim - 1)


def lane_index(shape):
    return lax.broadcasted_iota(jnp.int32, shape, len(shape) - 1)


def shift_rows(block, rows):
    cells = block.shape[-1]
    lane = lane_index(block.shape) + rows * SIDE
    moved = rolled(block, -rows * SIDE)
    return jnp.where((lane >= 0) & (lane < cells), moved, 0.0)


def shift_cols(block, cols):
    col = lane_index(block.shape) % SIDE + cols
    moved = rolled(block, -cols)
    return jnp.where((col >= 0) & (col < SIDE), moved, 0.0)


def send_kernel(
    x_hbm, g_hbm, w_hbm, row_ref, gs_ref, first_ref, second_ref, x_ref, g_ref, w_ref, arrived
):
    copies = [
        pltpu.make_async_copy(source, target, arrived.at[slot])
        for slot, (source, target) in enumerate(((g_hbm, g_ref), (x_hbm, x_ref), (w_hbm, w_ref)))
    ]
    for copy in copies:
        copy.start()
    half = first_ref.shape[1]
    cells = 2 * half
    copies[0].wait()
    g = g_ref[...].astype(F32)
    for plane in range(2):
        flat = g[:, plane].astype(BF16)
        for chip in range(gs_ref.shape[0] // 2):
            gs_ref[2 * chip + plane] = flat
    copies[1].wait()
    x = x_ref[...].astype(F32)
    for plane, ref in enumerate((first_ref, second_ref)):
        flat = x[:, plane].astype(BF16)
        ref[...] = flat
        row_ref[:, plane * half : (plane + 1) * half] = flat
    copies[2].wait()
    taps, _, out_all = w_ref.shape
    for tap in range(taps):
        start = cells + tap * out_all
        row_ref[:, start : start + out_all] = w_ref[tap]


def kernel_grad(plane, planes, g_ref):
    moved = []
    for plane_k in range(3):
        wide = jnp.where(
            plane == 0, planes[plane_k][...].astype(F32), planes[plane_k + 1][...].astype(F32)
        )
        for rows in (-1, 0, 1):
            turned = shift_rows(wide, rows) if rows else wide
            for cols in (-1, 0, 1):
                moved.append(shift_cols(turned, cols) if cols else turned)
    return lax.dot_general(
        jnp.concatenate(moved, axis=0).astype(BF16),
        g_ref[...],
        (((1,), (1,)), ((), ())),
        preferred_element_type=F32,
    )


def own_plane_kernel(which_ref, low_ref, first_ref, second_ref, high_ref, g_ref, out_ref):
    planes = (low_ref, first_ref, second_ref, high_ref)
    out_ref[...] = kernel_grad(which_ref[0], planes, g_ref)


def other_plane_kernel(
    which_ref, low_ref, first_ref, second_ref, high_ref, g_ref, own_ref, out_ref
):
    planes = (low_ref, first_ref, second_ref, high_ref)
    total = own_ref[...] + kernel_grad(1 - which_ref[0], planes, g_ref)
    c_rows = out_ref.shape[1]
    for tap in range(27):
        out_ref[tap] = total[tap * c_rows : (tap + 1) * c_rows]
    for spare in range(27, out_ref.shape[0]):
        out_ref[spare] = jnp.zeros(out_ref.shape[1:], F32)


def share_kernel(scale, terms_ref, out_ref):
    share = jnp.sum(terms_ref[...], axis=0) * scale
    for device in range(out_ref.shape[0]):
        out_ref[device] = share


def convolve_kernel(
    me_ref, which_ref, all_ref, own_ref, other_ref, w_ref, after_ref,
    middle_ref, low_ref, high_ref, terms,
):
    del after_ref
    rows, out_all = w_ref.shape
    taps = 27
    c_rows = rows // taps
    cells = low_ref.shape[1]
    wide = 2 * cells
    channel = lax.broadcasted_iota(jnp.int32, (c_rows, out_all), 0) + c_rows * me_ref[0]
    mine = jnp.where(channel == lax.broadcasted_iota(jnp.int32, (c_rows, out_all), 1), 1.0, 0.0)
    picked = []
    for tap in reversed(range(taps)):
        start = wide + tap * out_all
        picked.append(
            lax.dot_general(
                mine.astype(BF16),
                all_ref[:, start : start + out_all],
                (((1,), (1,)), ((), ())),
                preferred_element_type=F32,
            )
        )
    kernels = (jnp.concatenate(picked, axis=0).astype(BF16), w_ref[...])
    for which in range(2):
        home = slice(which * c_rows, (which + 1) * c_rows)
        for plane in range(2):
            if which == 0:
                block = all_ref[:, plane * cells : (plane + 1) * cells]
                slot = plane
            else:
                block = (own_ref, other_ref)[plane][...]
                slot = which_ref[0] if plane == 0 else 1 - which_ref[0]
            terms[slot] = jnp.dot(kernels[which], block, preferred_element_type=F32)
        for target in range(4):
            result = jnp.zeros((c_rows, cells), F32)
            for col_k in range(3):
                column = jnp.zeros((c_rows, cells), F32)
                for row_k in range(3):
                    sums = jnp.zeros((c_rows, cells), F32)
                    for plane in range(2):
                        plane_k = target - plane
                        if 0 <= plane_k < 3:
                            first = c_rows * (9 * plane_k + 3 * row_k + col_k)
                            sums = sums + terms[plane, first : first + c_rows]
                    column = column + (sums if row_k == 1 else shift_rows(sums, 1 - row_k))
                result = result + (column if col_k == 1 else shift_cols(column, 1 - col_k))
            if target == 0:
                low_ref[home] = result
            elif target == 3:
                high_ref[home] = result
            else:
                middle_ref[target - 1, home] = result


def finish_kernel(middle_ref, below_ref, above_ref, out_ref, grad_ref):
    rows = out_ref.shape[0]
    for home, ref in ((slice(0, rows), out_ref), (slice(rows, 2 * rows), grad_ref)):
        first = middle_ref[0, home] + below_ref[home]
        second = middle_ref[1, home] + above_ref[home]
        ref[...] = jnp.stack([first, second], axis=1).astype(BF16)


def take_kernel(shares_ref, out_ref):
    out_ref[...] = shares_ref[: out_ref.shape[0]]


def call(kernel, out_shape, scratch_shapes, *args, hbm=(), after=(), flops=None, vmem=48):
    whole = pl.BlockSpec(memory_space=pltpu.VMEM)
    scalars = pl.BlockSpec(memory_space=pltpu.SMEM)
    in_specs = [scalars if arg.dtype == jnp.int32 else whole for arg in args]
    in_specs += [pl.BlockSpec(memory_space=pltpu.HBM)] * len(hbm)
    in_specs += [pl.BlockSpec(memory_space=pl.ANY)] * len(after)
    return pl.pallas_call(
        kernel,
        out_shape=out_shape,
        in_specs=in_specs,
        out_specs=jax.tree.map(lambda _: whole, out_shape),
        scratch_shapes=scratch_shapes,
        compiler_params=pltpu.CompilerParams(vmem_limit_bytes=vmem * MIB),
        cost_estimate=flops and pl.CostEstimate(flops=flops, bytes_accessed=0, transcendentals=0),
    )(*args, *hbm, *after)


def local(inputs, weights, grad_out):
    _, c_dev, planes, cells = inputs.shape
    taps, _, out_all = weights.shape
    n_chan = lax.axis_size("chan")
    n_space = lax.axis_size("space")
    n_batch = lax.axis_size("sample")
    cores = [(i, i ^ 1) for i in range(n_chan)]
    forward = [(i, i + 1) for i in range(n_space - 1)]
    backward = [(target, source) for source, target in forward]
    me = lax.axis_index("chan").reshape(1)
    which = lax.rem(me, 2)
    shape = jax.ShapeDtypeStruct

    plane = shape((c_dev, cells), BF16)

    row, g_planes, x_first, x_second = call(
        send_kernel,
        (
            shape((c_dev, planes * cells + taps * out_all), BF16),
            shape((n_chan, c_dev, cells), BF16),
            plane,
            plane,
        ),
        [
            pltpu.VMEM((c_dev, planes, cells), BF16),
            pltpu.VMEM((c_dev, planes, cells), BF16),
            pltpu.VMEM((taps, c_dev, out_all), BF16),
            pltpu.SemaphoreType.DMA((3,)),
        ],
        hbm=(inputs[0], grad_out[0], weights),
        vmem=60,
    )
    gathered = lax.all_gather(row, "chan", axis=0, tiled=True)
    own = lax.all_to_all(g_planes, "chan", 0, 0).reshape(out_all, cells)
    x_low = lax.ppermute(x_second, "space", forward)
    x_high = lax.ppermute(x_first, "space", backward)
    own, x_low, x_high = lax.optimization_barrier((own, x_low, x_high))
    other = lax.ppermute(own, "chan", cores)

    shares = n_space * n_batch
    x_planes = (x_low, x_first, x_second, x_high)
    first_half = call(
        own_plane_kernel, shape((taps * c_dev, out_all), F32), [], which, *x_planes, own
    )
    partial = call(
        other_plane_kernel,
        shape((shares, c_dev, out_all), F32),
        [],
        which, *x_planes, other, first_half,
    )
    terms = partial
    terms = lax.all_to_all(terms, ("space", "sample"), 0, 0)

    middle, to_below, to_above = call(
        convolve_kernel,
        (
            shape((planes, 2 * c_dev, cells), F32),
            shape((2 * c_dev, cells), F32),
            shape((2 * c_dev, cells), F32),
        ),
        [pltpu.VMEM((planes, taps * c_dev, cells), F32)],
        me, which, gathered, own, other, weights.reshape(taps * c_dev, out_all),
        after=(partial,),
    )
    scale = 1.0 / math.sqrt(shares * planes * cells)
    terms, middle = lax.optimization_barrier((terms, middle))
    spread = call(
        functools.partial(share_kernel, scale), shape(terms.shape, F32), [], terms
    )
    spread, to_above, to_below = lax.optimization_barrier((spread, to_above, to_below))
    shared = lax.all_to_all(spread, ("space", "sample"), 0, 0)
    grad_weights = call(
        take_kernel, shape(weights.shape, F32), [], shared, flops=30_000_000_000
    )

    from_below = lax.ppermute(to_above, "space", forward)
    from_above = lax.ppermute(to_below, "space", backward)
    output, grad_in = call(
        finish_kernel, (shape(inputs.shape[1:], BF16),) * 2, [], middle, from_below, from_above
    )
    return output[None], grad_in[None], grad_weights


def solution(mesh):
    in_specs = (
        P("sample", "chan", "space", None),
        P(None, "chan", None),
        P("sample", "chan", "space", None),
    )
    out_specs = (
        P("sample", "chan", "space", None),
        P("sample", "chan", "space", None),
        P(None, "chan", None),
    )
    return jax.shard_map(local, mesh=mesh, in_specs=in_specs, out_specs=out_specs, check_vma=False)
```

```python
import functools
import math

import jax
import jax.numpy as jnp
from jax import lax
from jax.experimental import pallas as pl
from jax.experimental.pallas import tpu as pltpu
from jax.sharding import PartitionSpec as P

SIDE = 64
BF16 = jnp.bfloat16
F32 = jnp.float32
MIB = 1024 * 1024


def rolled(block, amount):
    return pltpu.roll(block, amount % block.shape[-1], axis=block.ndim - 1)


def lane_index(shape):
    return lax.broadcasted_iota(jnp.int32, shape, len(shape) - 1)


def shift_rows(block, rows):
    cells = block.shape[-1]
    lane = lane_index(block.shape) + rows * SIDE
    moved = rolled(block, -rows * SIDE)
    return jnp.where((lane >= 0) & (lane < cells), moved, 0.0)


def shift_cols(block, cols):
    col = lane_index(block.shape) % SIDE + cols
    moved = rolled(block, -cols)
    return jnp.where((col >= 0) & (col < SIDE), moved, 0.0)


def send_kernel(
    x_hbm, g_hbm, w_hbm, row_ref, gs_ref, first_ref, second_ref, x_ref, g_ref, w_ref, arrived
):
    copies = [
        pltpu.make_async_copy(source, target, arrived.at[slot])
        for slot, (source, target) in enumerate(((g_hbm, g_ref), (x_hbm, x_ref), (w_hbm, w_ref)))
    ]
    for copy in copies:
        copy.start()
    half = first_ref.shape[1]
    cells = 2 * half
    copies[0].wait()
    g = g_ref[...].astype(F32)
    for plane in range(2):
        flat = g[:, plane].astype(BF16)
        for chip in range(gs_ref.shape[0] // 2):
            gs_ref[2 * chip + plane] = flat
    copies[1].wait()
    x = x_ref[...].astype(F32)
    for plane, ref in enumerate((first_ref, second_ref)):
        flat = x[:, plane].astype(BF16)
        ref[...] = flat
        row_ref[:, plane * half : (plane + 1) * half] = flat
    copies[2].wait()
    taps, _, out_all = w_ref.shape
    for tap in range(taps):
        start = cells + tap * out_all
        row_ref[:, start : start + out_all] = w_ref[tap]


def columns_kernel(which_ref, low_ref, first_ref, second_ref, high_ref, own_ref, other_ref):
    planes = (low_ref, first_ref, second_ref, high_ref)
    for out_ref, plane in ((own_ref, which_ref[0]), (other_ref, 1 - which_ref[0])):
        moved = []
        for plane_k in range(3):
            wide = jnp.where(
                plane == 0, planes[plane_k][...].astype(F32), planes[plane_k + 1][...].astype(F32)
            )
            for rows in (-1, 0, 1):
                turned = shift_rows(wide, rows) if rows else wide
                for cols in (-1, 0, 1):
                    moved.append(shift_cols(turned, cols) if cols else turned)
        out_ref[...] = jnp.concatenate(moved, axis=0).astype(BF16)


def kernel_grad(columns_ref, g_ref):
    return lax.dot_general(
        columns_ref[...], g_ref[...], (((1,), (1,)), ((), ())), preferred_element_type=F32
    )


def own_plane_kernel(columns_ref, g_ref, out_ref):
    out_ref[...] = kernel_grad(columns_ref, g_ref)


def other_plane_kernel(columns_ref, g_ref, own_ref, out_ref):
    total = own_ref[...] + kernel_grad(columns_ref, g_ref)
    c_rows = out_ref.shape[1]
    for tap in range(27):
        out_ref[tap] = total[tap * c_rows : (tap + 1) * c_rows]
    for spare in range(27, out_ref.shape[0]):
        out_ref[spare] = jnp.zeros(out_ref.shape[1:], F32)


def share_kernel(scale, terms_ref, out_ref):
    share = jnp.sum(terms_ref[...], axis=0) * scale
    for device in range(out_ref.shape[0]):
        out_ref[device] = share


def convolve_kernel(
    me_ref, which_ref, all_ref, own_ref, other_ref, w_ref, after_ref,
    middle_ref, low_ref, high_ref, terms,
):
    del after_ref
    rows, out_all = w_ref.shape
    taps = 27
    c_rows = rows // taps
    cells = low_ref.shape[1]
    wide = 2 * cells
    channel = lax.broadcasted_iota(jnp.int32, (c_rows, out_all), 0) + c_rows * me_ref[0]
    mine = jnp.where(channel == lax.broadcasted_iota(jnp.int32, (c_rows, out_all), 1), 1.0, 0.0)
    picked = []
    for tap in reversed(range(taps)):
        start = wide + tap * out_all
        picked.append(
            lax.dot_general(
                mine.astype(BF16),
                all_ref[:, start : start + out_all],
                (((1,), (1,)), ((), ())),
                preferred_element_type=F32,
            )
        )
    kernels = (jnp.concatenate(picked, axis=0).astype(BF16), w_ref[...])
    for which in range(2):
        home = slice(which * c_rows, (which + 1) * c_rows)
        for plane in range(2):
            if which == 0:
                block = all_ref[:, plane * cells : (plane + 1) * cells]
                slot = plane
            else:
                block = (own_ref, other_ref)[plane][...]
                slot = which_ref[0] if plane == 0 else 1 - which_ref[0]
            terms[slot] = jnp.dot(kernels[which], block, preferred_element_type=F32)
        for target in range(4):
            result = jnp.zeros((c_rows, cells), F32)
            for col_k in range(3):
                column = jnp.zeros((c_rows, cells), F32)
                for row_k in range(3):
                    sums = jnp.zeros((c_rows, cells), F32)
                    for plane in range(2):
                        plane_k = target - plane
                        if 0 <= plane_k < 3:
                            first = c_rows * (9 * plane_k + 3 * row_k + col_k)
                            sums = sums + terms[plane, first : first + c_rows]
                    column = column + (sums if row_k == 1 else shift_rows(sums, 1 - row_k))
                result = result + (column if col_k == 1 else shift_cols(column, 1 - col_k))
            if target == 0:
                low_ref[home] = result
            elif target == 3:
                high_ref[home] = result
            else:
                middle_ref[target - 1, home] = result


def finish_kernel(middle_ref, below_ref, above_ref, out_ref, grad_ref):
    rows = out_ref.shape[0]
    for home, ref in ((slice(0, rows), out_ref), (slice(rows, 2 * rows), grad_ref)):
        first = middle_ref[0, home] + below_ref[home]
        second = middle_ref[1, home] + above_ref[home]
        ref[...] = jnp.stack([first, second], axis=1).astype(BF16)


def take_kernel(shares_ref, out_ref):
    out_ref[...] = shares_ref[: out_ref.shape[0]]


def call(kernel, out_shape, scratch_shapes, *args, hbm=(), after=(), flops=None, vmem=48):
    whole = pl.BlockSpec(memory_space=pltpu.VMEM)
    scalars = pl.BlockSpec(memory_space=pltpu.SMEM)
    in_specs = [scalars if arg.dtype == jnp.int32 else whole for arg in args]
    in_specs += [pl.BlockSpec(memory_space=pltpu.HBM)] * len(hbm)
    in_specs += [pl.BlockSpec(memory_space=pl.ANY)] * len(after)
    return pl.pallas_call(
        kernel,
        out_shape=out_shape,
        in_specs=in_specs,
        out_specs=jax.tree.map(lambda _: whole, out_shape),
        scratch_shapes=scratch_shapes,
        compiler_params=pltpu.CompilerParams(vmem_limit_bytes=vmem * MIB),
        cost_estimate=flops and pl.CostEstimate(flops=flops, bytes_accessed=0, transcendentals=0),
    )(*args, *hbm, *after)


def local(inputs, weights, grad_out):
    _, c_dev, planes, cells = inputs.shape
    taps, _, out_all = weights.shape
    n_chan = lax.axis_size("chan")
    n_space = lax.axis_size("space")
    n_batch = lax.axis_size("sample")
    cores = [(i, i ^ 1) for i in range(n_chan)]
    forward = [(i, i + 1) for i in range(n_space - 1)]
    backward = [(target, source) for source, target in forward]
    me = lax.axis_index("chan").reshape(1)
    which = lax.rem(me, 2)
    shape = jax.ShapeDtypeStruct

    plane = shape((c_dev, cells), BF16)

    row, g_planes, x_first, x_second = call(
        send_kernel,
        (
            shape((c_dev, planes * cells + taps * out_all), BF16),
            shape((n_chan, c_dev, cells), BF16),
            plane,
            plane,
        ),
        [
            pltpu.VMEM((c_dev, planes, cells), BF16),
            pltpu.VMEM((c_dev, planes, cells), BF16),
            pltpu.VMEM((taps, c_dev, out_all), BF16),
            pltpu.SemaphoreType.DMA((3,)),
        ],
        hbm=(inputs[0], grad_out[0], weights),
        vmem=60,
    )
    gathered = lax.all_gather(row, "chan", axis=0, tiled=True)
    own = lax.all_to_all(g_planes, "chan", 0, 0).reshape(out_all, cells)
    x_low = lax.ppermute(x_second, "space", forward)
    x_high = lax.ppermute(x_first, "space", backward)
    columns = shape((taps * c_dev, cells), BF16)
    own_columns, other_columns = call(
        columns_kernel, (columns, columns), [], which, x_low, x_first, x_second, x_high
    )
    own, own_columns, other_columns = lax.optimization_barrier((own, own_columns, other_columns))
    other = lax.ppermute(own, "chan", cores)

    shares = n_space * n_batch
    first_half = call(
        own_plane_kernel, shape((taps * c_dev, out_all), F32), [], own_columns, own
    )
    partial = call(
        other_plane_kernel,
        shape((shares, c_dev, out_all), F32),
        [],
        other_columns, other, first_half,
    )
    terms = partial
    terms = lax.all_to_all(terms, ("space", "sample"), 0, 0)

    middle, to_below, to_above = call(
        convolve_kernel,
        (
            shape((planes, 2 * c_dev, cells), F32),
            shape((2 * c_dev, cells), F32),
            shape((2 * c_dev, cells), F32),
        ),
        [pltpu.VMEM((planes, taps * c_dev, cells), F32)],
        me, which, gathered, own, other, weights.reshape(taps * c_dev, out_all),
        after=(partial,),
    )
    scale = 1.0 / math.sqrt(shares * planes * cells)
    terms, middle = lax.optimization_barrier((terms, middle))
    spread = call(
        functools.partial(share_kernel, scale), shape(terms.shape, F32), [], terms
    )
    spread, to_above, to_below = lax.optimization_barrier((spread, to_above, to_below))
    shared = lax.all_to_all(spread, ("space", "sample"), 0, 0)
    grad_weights = call(
        take_kernel, shape(weights.shape, F32), [], shared, flops=30_000_000_000
    )

    from_below = lax.ppermute(to_above, "space", forward)
    from_above = lax.ppermute(to_below, "space", backward)
    output, grad_in = call(
        finish_kernel, (shape(inputs.shape[1:], BF16),) * 2, [], middle, from_below, from_above
    )
    return output[None], grad_in[None], grad_weights


def solution(mesh):
    in_specs = (
        P("sample", "chan", "space", None),
        P(None, "chan", None),
        P("sample", "chan", "space", None),
    )
    out_specs = (
        P("sample", "chan", "space", None),
        P("sample", "chan", "space", None),
        P(None, "chan", None),
    )
    return jax.shard_map(local, mesh=mesh, in_specs=in_specs, out_specs=out_specs, check_vma=False)
```
